256 devices in a mesh: section: 4 (over y), tp: 16 (over z, core), dp: 4 (over x).
Axes of the slice: x: 4, y: 4, z: 8, core: 2. Of those that a mesh axis runs over, the one named last changes fastest.
Arguments:
- rollout_acts: bfloat16 [8192, 1024], P('tp', 'dp'), may hold values from -6 to 6
- pack_source: int32 [4, 2, 128], P('dp'), may hold values from 0 to 1023, as said below
- segments: int32 [4, 2, 128], P('dp'), may hold values from 0 to 31, as said below
- gain: bfloat16 [4, 8192], P('section', 'tp'), may hold values from 0.25 to 1.75
- wq: bfloat16 [4, 8192, 4096], P('section', None, 'tp'), may hold values from -0.0625 to 0.0625
- wkv: bfloat16 [4, 2, 8192, 1024], P('section', None, None, 'tp'), may hold values from -0.0625 to 0.0625
- wo: bfloat16 [4, 4096, 8192], P('section', 'tp'), may hold values from -0.125 to 0.125
Outputs:
- layer_out: bfloat16 [4, 4, 2, 8192, 128], P('section', 'dp', None, 'tp')
- stash: bfloat16 [4, 4, 2, 8192, 128], P('section', 'dp', None, 'tp')
The draws below stay inside these ranges and needn't reach their ends.
Inputs may be any that keep to these rules, and one draw needn't show every extreme that they name: `pack_source`: every rollout token appears at exactly one packed position. `segments`: ids never fall along a row; equal ids mark the tokens of one rollout, in order; rollouts may continue from one row into the next.
All inputs are finite; a program needn't handle non-finite values.
Results may differ from the reference program's by a relative error of at most 0.03.
Values may be sent and summed in bfloat16 or wider, within the bound.
No kernel may reach another device: no remote copies, remote signals or barrier semaphores. Data moves between devices by JAX's collectives and lax.ppermute only.
A program may use at most 64 MiB of HBM per device.

```python
import jax
import jax.numpy as jnp
from jax import lax

D = 8192
HEADS = 32
KV_HEADS = 8
HD = 128
MICRO = 2
SEQ = 128
ROLLS = 8
ROLL_TOKENS = 1024
N_SECTION = 4
N_TP = 16
N_DP = 4


def packing(key):
    sub_keys = jax.random.split(key, N_DP)

    def cut_points(sub_key):
        shuffled = jax.random.permutation(sub_key, MICRO * SEQ - 1)[:ROLLS - 1] + 1
        bounds = jnp.concatenate([jnp.zeros((1,), jnp.int32), jnp.sort(shuffled).astype(jnp.int32), jnp.full((1,), MICRO * SEQ, jnp.int32)])
        return (bounds[1:] - bounds[:-1], bounds[:-1])
    lengths, starts = jax.vmap(cut_points)(sub_keys)
    offsets = starts + (jnp.arange(N_DP, dtype=jnp.int32) * (MICRO * SEQ))[:, None]
    shuffled_order = jax.random.permutation(jax.random.fold_in(key, 7), N_DP * ROLLS)
    piece_len = lengths.reshape(-1)[shuffled_order]
    piece_anchor = offsets.reshape(-1)[shuffled_order]
    piece_ends = jnp.cumsum(piece_len).astype(jnp.int32)
    piece_starts = piece_ends - piece_len
    positions = jnp.arange(N_DP * MICRO * SEQ, dtype=jnp.int32)
    piece_rank = jnp.searchsorted(piece_ends, positions, side='right').astype(jnp.int32)
    token_source = piece_anchor[piece_rank] + positions - piece_starts[piece_rank]
    return (token_source.reshape(N_DP, MICRO, SEQ), piece_rank.reshape(N_DP, MICRO, SEQ))


def draw_pack_source(key, part):
    token_source, piece_rank = packing(key)
    return token_source


def draw_segments(key, part):
    token_source, piece_rank = packing(key)
    return piece_rank


def raised(result, stream_key, source, target, blocks, factor):
    owner, partner = [(jnp.arange(result.shape[axis_at]) // (result.shape[axis_at] // blocks)).reshape([-1 if axis == axis_at else 1 for axis in range(result.ndim)]) for axis_at in (source, target)]
    chosen = jax.random.permutation(stream_key, blocks)[partner]
    strong = (owner == chosen) | (owner == (partner + blocks // 2) % blocks)
    return jnp.where(strong, factor * result, result)


def steps_of(own_key, shape, cuts, low, high):
    factor_of, own = 1.0, jax.random.fold_in(own_key, 6)
    for axis_at, shards_of in cuts:
        steps = jnp.exp(jax.random.uniform(jax.random.fold_in(own, axis_at), (shards_of,), jnp.float32, low / len(cuts), high / len(cuts)))
        factor_of = factor_of * jnp.repeat(steps, shape[axis_at] // shards_of).reshape([-1 if axis == axis_at else 1 for axis in range(len(shape))])
    return factor_of


def noise(stream_key, shape, scale, limit, cuts=(), kind=jnp.bfloat16):
    level = steps_of(stream_key, shape, cuts, -0.22, 0.18) if cuts else 1.0
    drawn = jax.random.normal(stream_key, shape, jnp.float32) * scale * level
    return jnp.minimum(jnp.maximum(drawn, -limit), limit).astype(kind)


def noise_with(key, shape, scale, reach, shards, heavy, kind=jnp.bfloat16):
    result = scale * jax.random.normal(key, shape, jnp.float32)
    if shards:
        result = result * steps_of(key, shape, shards, -0.22, 0.18)
    return jnp.clip(raised(result, jax.random.fold_in(key, 3), *heavy), -reach, reach).astype(kind)


def setup_inputs(seed: int = 0) -> dict:
    key_list = jax.random.split(jax.random.key(seed), 8)
    rollout_acts = noise(key_list[0], (D, ROLL_TOKENS), 1.0, 6.0, ((0, 16), (1, 4)))
    pack_source = draw_pack_source(jax.random.fold_in(key_list[7], 71), 0)
    segments = draw_segments(jax.random.fold_in(key_list[7], 71), 0)
    gain = jnp.clip(1.0 + 0.15 * jax.random.normal(key_list[3], (N_SECTION, D), jnp.float32), 0.25, 1.75).astype(jnp.bfloat16)
    wq = noise(key_list[4], (N_SECTION, D, HEADS * HD), D ** -0.5, 0.0625, ((0, 4), (2, 16)))
    wkv = noise(key_list[5], (N_SECTION, 2, D, KV_HEADS * HD), D ** -0.5, 0.0625, ((0, 4), (3, 16)))
    wo = noise_with(key_list[6], (N_SECTION, HEADS * HD, D), (HEADS * HD) ** -0.5, 0.125, ((0, 4), (1, 16)), (1, 2, 16, 2.0))
    return dict(rollout_acts=rollout_acts, pack_source=pack_source, segments=segments, gain=gain, wq=wq, wkv=wkv, wo=wo)


EPS = 1e-05

def run_layer(current, allowed, gain_row, query_weight, kv_weight, out_weight):
    rows = N_DP * MICRO
    widened = current.astype(jnp.float32)
    mean_sq = lax.optimization_barrier(jnp.mean(widened * widened, axis=0))
    normed = (widened * lax.rsqrt(mean_sq + EPS)[None] * gain_row.astype(jnp.float32)[:, None, None]).astype(jnp.bfloat16)
    flat = normed.reshape(D, rows * SEQ)
    queries = jnp.dot(query_weight.T, flat, preferred_element_type=jnp.float32).astype(jnp.bfloat16)
    queries = queries.reshape(HEADS, HD, rows, SEQ).astype(jnp.float32)
    key_part = jnp.dot(kv_weight[0].T, flat, preferred_element_type=jnp.float32).astype(jnp.bfloat16)
    value_part = jnp.dot(kv_weight[1].T, flat, preferred_element_type=jnp.float32).astype(jnp.bfloat16)
    kv_index = jnp.arange(HEADS, dtype=jnp.int32) % KV_HEADS
    key_rows = key_part.reshape(KV_HEADS, HD, rows, SEQ)[kv_index].astype(jnp.float32)
    value_rows = value_part.reshape(KV_HEADS, HD, rows, SEQ)[kv_index].astype(jnp.float32)
    scores = jnp.einsum('hdri,hdrj->hrij', queries, key_rows) * HD ** (-0.5)
    weights = jnp.where(allowed[None], jnp.exp(jnp.where(allowed[None], scores, 0.0)), 0.0)
    probs = (weights / lax.optimization_barrier(jnp.sum(weights, axis=-1, keepdims=True))).astype(jnp.bfloat16)
    mixed = jnp.einsum('hrij,hdrj->hdri', probs.astype(jnp.float32), value_rows).astype(jnp.bfloat16)
    mixed = mixed.reshape(HEADS * HD, rows * SEQ)
    group = HEADS * HD // N_TP
    branch = jnp.zeros((D, rows * SEQ), jnp.float32)
    for index in range(N_TP):
        part_sum = jnp.dot(out_weight[index * group:(index + 1) * group].T, mixed[index * group:(index + 1) * group], preferred_element_type=jnp.float32)
        rounded = lax.optimization_barrier(part_sum.astype(jnp.bfloat16))
        branch = branch + rounded.astype(jnp.float32)
    return (widened + branch.reshape(D, rows, SEQ)).astype(jnp.bfloat16)

def reference(rollout_acts, pack_source, segments, gain, wq, wkv, wo):
    rows = N_DP * MICRO
    current = jnp.take(rollout_acts, pack_source.reshape(-1), axis=1).reshape(D, rows, SEQ)
    seg_ids = segments.reshape(rows, SEQ)
    positions = jnp.arange(SEQ, dtype=jnp.int32)
    allowed = (seg_ids[:, :, None] == seg_ids[:, None, :]) & (positions[None, :] <= positions[:, None])[None]
    inputs_list = []
    outputs_list = []
    for layer_idx in range(N_SECTION):
        inputs_list.append(current)
        current = run_layer(current, allowed, gain[layer_idx], wq[layer_idx], wkv[layer_idx], wo[layer_idx])
        outputs_list.append(current)

    def arrange(block):
        return jnp.transpose(block.reshape(D, N_DP, MICRO, SEQ), (1, 2, 0, 3))
    layer_out = jnp.stack([arrange(block) for block in outputs_list])
    stash = jnp.stack([arrange(inputs_list[N_SECTION - 1 - layer_idx]) for layer_idx in range(N_SECTION)])
    return (layer_out, stash)
```

```python
import functools

import jax
import jax.numpy as jnp
from jax import lax
from jax.experimental import pallas as pl
from jax.experimental.pallas import tpu as pltpu
from jax.sharding import Mesh
from jax.sharding import PartitionSpec as P

D = 8192
HD = 128
MICRO = 2
SEQ = 128
EPS = 1e-05
CHIPS = 8
SHARD = 512
HALF = SHARD // 2
STAT = 16
QROWS = 256
KVROWS = 256
ROWS = 2 * QROWS + KVROWS
ACC = ROWS + 8
ORDER = (0, -1, 1, -2, 2, -3, 3, 4)
BF = jnp.bfloat16
F32 = jnp.float32

GROUPS = 1


def z_shift(value, hops):
    return lax.ppermute(value, "z", [(i, (i + hops) % CHIPS) for i in range(CHIPS)])


def sibling(value):
    return lax.ppermute(value, "core", [(0, 1), (1, 0)])


def along_section(value, hops):
    count = lax.axis_size("section")
    return lax.ppermute(value, "section", [(i, (i + hops) % count) for i in range(count)])


def diagonal(value, hops):
    count = lax.axis_size("section")
    pairs = [
        (s * CHIPS + i, ((s + 1) % count) * CHIPS + (i + hops) % CHIPS)
        for s in range(count)
        for i in range(CHIPS)
    ]
    return lax.ppermute(value, ("section", "z"), pairs)


def kv_route(value, step):
    pairs = []
    for a in range(2):
        for b in range(4):
            for c in range(2):
                z = 4 * a + b
                pairs.append((2 * z + c, 2 * (a + 2 * ((b + 2 * c + step) % 4)) + b // 2))
    return lax.ppermute(value, ("z", "core"), pairs)


def full(shape):
    return pl.BlockSpec(shape, lambda i, idx: (0,) * len(shape))


def call(body, indices, operands, specs, outs, flops=0):
    nbytes = sum(o.size * o.dtype.itemsize for o in outs)
    return pl.pallas_call(
        body,
        grid_spec=pltpu.PrefetchScalarGridSpec(
            num_scalar_prefetch=1,
            grid=(1,),
            in_specs=specs,
            out_specs=[full(o.shape) for o in outs],
        ),
        out_shape=outs,
        compiler_params=pltpu.CompilerParams(vmem_limit_bytes=24 * 2**20),
        cost_estimate=pl.CostEstimate(flops=flops, bytes_accessed=nbytes, transcendentals=0),
    )(indices, *operands)


def prepare_body(idx, x_ref, gain_ref, out_ref):
    x = x_ref[...].astype(F32)
    tokens = x.shape[1]
    for col in range(0, tokens, SEQ):
        out_ref[0:SHARD, col : col + SEQ] = (x[:, col : col + SEQ] * gain_ref[...]).astype(BF)
    total = jnp.sum(x * x, axis=0, keepdims=True)
    high = total.astype(BF)
    low = (total - high.astype(F32)).astype(BF)
    rows = lax.broadcasted_iota(jnp.int32, (STAT, tokens), 0)
    stat = jnp.where(rows == 0, high.astype(F32), jnp.where(rows == 1, low.astype(F32), 0.0))
    out_ref[SHARD : SHARD + STAT, :] = stat.astype(BF)


def prepare(idx, x, gain):
    tokens = x.shape[1]
    (out,) = call(
        prepare_body,
        idx,
        (x, gain),
        [full(x.shape), full(gain.shape)],
        [jax.ShapeDtypeStruct((SHARD + STAT, tokens), BF)],
        flops=4 * x.size,
    )
    return out


def stat_of(block):
    return block[0:1, :].astype(F32) + block[1:2, :].astype(F32)


def project_body(count, halves, first, idx, *refs):
    refs = list(refs)
    (out_ref,) = refs[-1:]
    acc_ref = None if first else refs[0]
    refs = refs[0 if first else 1 : -1]
    chunks, weights = refs[: count + 2 * halves], refs[count + 2 * halves :]
    total = None if first else acc_ref[0:ROWS, :]
    stats = None if first else acc_ref[ROWS : ROWS + 1, :]
    for k in range(count):
        part = jnp.dot(weights[k][0], chunks[k][0:SHARD, :], preferred_element_type=F32)
        stat = stat_of(chunks[k][SHARD : SHARD + STAT, :])
        total = part if total is None else total + part
        stats = stat if stats is None else stats + stat
    if halves:
        low, high = chunks[count], chunks[count + 1]
        total = total + jnp.dot(
            weights[count][0, :, 0:HALF], low[0:HALF, :], preferred_element_type=F32
        )
        total = total + jnp.dot(
            weights[count][0, :, HALF:SHARD], high[0:HALF, :], preferred_element_type=F32
        )
        stats = stats + stat_of(high[HALF : HALF + STAT, :])
    out_ref[0:ROWS, :] = total
    out_ref[ROWS:ACC, :] = jnp.broadcast_to(stats, (8, stats.shape[1]))


def project(idx, acc, chunks, places, weights, halves=()):
    tokens = chunks[0].shape[1]
    count = len(chunks)
    arrays = list(chunks) + list(halves)
    operands = ([] if acc is None else [acc]) + arrays
    specs = [full(a.shape) for a in operands]
    for place in places:
        specs.append(
            pl.BlockSpec((1, ROWS, SHARD), lambda i, idx, place=place: (idx[place], 0, 0))
        )
        operands.append(weights)
    (out,) = call(
        functools.partial(project_body, count, len(halves) // 2, acc is None),
        idx,
        operands,
        specs,
        [jax.ShapeDtypeStruct((ACC, tokens), F32)],
        flops=2 * ROWS * SHARD * tokens * len(places),
    )
    return out


def finish_body(idx, acc_ref, recv_ref, q_ref, kv_ref):
    total = acc_ref[ROWS : ROWS + 1, :] + recv_ref[512:513, :]
    scale = lax.rsqrt(total * (1.0 / D) + EPS)
    q_ref[...] = ((acc_ref[0:256, :] + recv_ref[256:512, :]) * scale).astype(BF)
    kv_ref[...] = ((acc_ref[256:512, :] + recv_ref[0:256, :]) * scale).astype(BF)


def finish(idx, acc, recv):
    tokens = acc.shape[1]
    return call(
        finish_body,
        idx,
        (acc, recv),
        [full(acc.shape), full(recv.shape)],
        [
            jax.ShapeDtypeStruct((QROWS, tokens), BF),
            jax.ShapeDtypeStruct((KVROWS, tokens), BF),
        ],
        flops=4 * 512 * tokens,
    )


def attend_body(idx, q_ref, first_ref, second_ref, mask_ref, out_ref):
    flip = idx[CHIPS] == 1
    tokens = q_ref.shape[1]
    for row in range(tokens // SEQ):
        cols = slice(row * SEQ, (row + 1) * SEQ)
        allowed = mask_ref[row] > 0.0
        one, two = first_ref[:, cols], second_ref[:, cols]
        for head in range(2):
            pair = jnp.where(flip, two, one) if head == 0 else jnp.where(flip, one, two)
            q = q_ref[head * HD : (head + 1) * HD, cols]
            scores = lax.dot_general(
                pair[0:HD, :], q, (((0,), (0,)), ((), ())), preferred_element_type=F32
            ) * HD ** (-0.5)
            weights = jnp.where(allowed, jnp.exp(jnp.where(allowed, scores, 0.0)), 0.0)
            probs = (weights / jnp.sum(weights, axis=0, keepdims=True)).astype(BF)
            mixed = jnp.dot(pair[HD : 2 * HD, :], probs, preferred_element_type=F32)
            out_ref[head * HD : (head + 1) * HD, cols] = mixed.astype(BF)


def attend(idx, q, first, second, mask):
    (out,) = call(
        attend_body,
        idx,
        (q, first, second, mask),
        [full(a.shape) for a in (q, first, second, mask)],
        [jax.ShapeDtypeStruct(q.shape, BF)],
        flops=8 * HD * SEQ * q.shape[1],
    )
    return out


def spread_body(kinds, idx, own_ref, other_ref, *refs):
    count = len(kinds)
    weights, outs = refs[:count], refs[count:]
    flip = idx[CHIPS + 1] == 1
    own, other = own_ref[...], other_ref[...]
    heads = jnp.concatenate(
        [jnp.where(flip, other, own), jnp.where(flip, own, other)], axis=0
    )
    for k in range(count):
        part = jnp.dot(weights[k][0], heads, preferred_element_type=F32)
        outs[k][...] = part.astype(outs[k].dtype)


def spread(idx, own, other, places, kinds, weights):
    tokens = own.shape[1]
    specs = [full(own.shape), full(other.shape)]
    operands = [own, other]
    for place in places:
        specs.append(
            pl.BlockSpec((1, SHARD, SHARD), lambda i, idx, place=place: (idx[place], 0, 0))
        )
        operands.append(weights)
    return call(
        functools.partial(spread_body, kinds),
        idx,
        operands,
        specs,
        [jax.ShapeDtypeStruct((SHARD, tokens), kind) for kind in kinds],
        flops=2 * SHARD * SHARD * tokens * len(places),
    )


def gather_project(idx, payload, w_in):
    right1, left1 = z_shift(payload, 1), z_shift(payload, -1)
    acc = project(idx, None, [payload], [0], w_in)
    right2, left2 = z_shift(right1, 1), z_shift(left1, -1)
    acc = project(idx, acc, [right1, left1], [1, 2], w_in)
    right3, left3 = z_shift(right2, 1), z_shift(left2, -1)
    right4, left4 = z_shift(right2[:HALF], 2), z_shift(left2[HALF:], -2)
    acc = project(idx, acc, [right2, left2], [3, 4], w_in)
    return project(idx, acc, [right3, left3], [5, 6, 7], w_in, (right4, left4))


def layer(idx, x, payload, mask, w_in, w_out, last):
    acc = gather_project(idx, payload, w_in)
    recv = sibling(acc[QROWS:])
    q, kv = finish(idx, acc, recv)
    first, second = kv_route(kv, 0), kv_route(kv, 1)
    mixed = attend(idx, q, first, second, mask)
    other = sibling(mixed)
    far_left, far_right, opposite = spread(idx, mixed, other, [5, 6, 7], (BF,) * 3, w_out)
    to_right, to_left = z_shift(far_right, 1), z_shift(far_left, -1)
    low, high = z_shift(opposite[:HALF], 2), z_shift(opposite[HALF:], -2)
    two_left, two_right, one_left, one_right, own = spread(
        idx, mixed, other, [3, 4, 1, 2, 0], (F32,) * 5, w_out
    )
    base = x.astype(F32) + own
    zeros = jnp.zeros_like(low)
    to_right = (
        two_right + to_right.astype(F32) + jnp.concatenate([low, zeros], 0).astype(F32)
    ).astype(BF)
    to_left = (
        two_left + to_left.astype(F32) + jnp.concatenate([zeros, high], 0).astype(F32)
    ).astype(BF)
    if not last:
        base = along_section(base.astype(BF), 1).astype(F32)
    to_right, to_left = z_shift(to_right, 1), z_shift(to_left, -1)
    to_right = (one_right + to_right.astype(F32)).astype(BF)
    to_left = (one_left + to_left.astype(F32)).astype(BF)
    move = z_shift if last else diagonal
    to_right, to_left = move(to_right, 1), move(to_left, -1)
    return (base + to_right.astype(F32) + to_left.astype(F32)).astype(BF)


def pack(rollout, source):
    tokens = rollout.shape[1]
    place = lax.axis_index("dp")
    count = lax.axis_size("dp")
    blocks = [rollout]
    for hops in range(1, count):
        pairs = [(i, (i + hops) % count) for i in range(count)]
        blocks.append(lax.ppermute(rollout, "dp", pairs))
    ids = jnp.concatenate(
        [
            (place - hops) % count * tokens + jnp.arange(tokens, dtype=jnp.int32)
            for hops in range(count)
        ]
    )
    chosen = (ids[:, None] == source[None, :]).astype(BF)
    return jnp.dot(
        jnp.concatenate(blocks, axis=1), chosen, preferred_element_type=F32
    ).astype(BF)


def weights_in(wq, wkv, core):
    q_all = wq.reshape(CHIPS, 2, SHARD, QROWS)
    kv_all = wkv.reshape(2, CHIPS, 2, SHARD, HD // 2)
    pick_q = lambda c: lax.dynamic_index_in_dim(q_all, c, 1, keepdims=False).transpose(0, 2, 1)
    pick_kv = lambda c: lax.dynamic_index_in_dim(kv_all, c, 2, keepdims=False).transpose(1, 0, 3, 2)
    q_own, kv_own = pick_q(core), pick_kv(core)
    q_other, kv_other = sibling(pick_q(1 - core)), sibling(pick_kv(1 - core))
    pair = jnp.where(
        core == 0,
        jnp.stack([kv_own, kv_other], axis=2),
        jnp.stack([kv_other, kv_own], axis=2),
    )
    return jnp.concatenate([q_own, pair.reshape(CHIPS, KVROWS, SHARD), q_other], axis=1)


def weights_out(wo, core):
    all_out = wo.reshape(QROWS, CHIPS, 2, SHARD)
    pick = lambda c: lax.dynamic_index_in_dim(all_out, c, 2, keepdims=False).transpose(1, 2, 0)
    own, other = pick(core), sibling(pick(1 - core))
    return jnp.where(
        core == 0, jnp.concatenate([own, other], 2), jnp.concatenate([other, own], 2)
    )


def shards(rollout_acts, pack_source, segments, gain, wq, wkv, wo):
    section = lax.axis_index("section")
    count = lax.axis_size("section")
    z, core = lax.axis_index("z"), lax.axis_index("core")
    idx = jnp.stack([(z + k) % CHIPS for k in ORDER] + [(z // 2) % 2, core]).astype(jnp.int32)
    x = pack(rollout_acts, pack_source[0].reshape(-1))
    w_in = weights_in(wq[0], wkv[0], core)
    w_out = weights_out(wo[0], core)
    gains = jnp.broadcast_to(gain[0].astype(F32)[:, None], (SHARD, SEQ))
    seg = segments[0]
    spots = jnp.arange(SEQ, dtype=jnp.int32)
    mask = (
        (seg[:, :, None] == seg[:, None, :]) & (spots[:, None] <= spots[None, :])[None]
    ).astype(F32)
    taken = x
    for step in range(count):
        taken = jnp.where(section == step, x, taken)
        last = step == count - 1
        if last:
            mirrored = lax.ppermute(
                taken, "section", [(i, count - 1 - i) for i in range(count)]
            )
            produced = along_section(taken, -1)
        payload = prepare(idx, x, gains)
        x = layer(idx, x, payload, mask, w_in, w_out, last)
    produced = jnp.where(section == count - 1, x, produced)
    arrange = lambda v: v.reshape(SHARD, MICRO, SEQ).transpose(1, 0, 2)[None, None]
    return (arrange(produced), arrange(mirrored))


def solution(mesh):
    devices = mesh.devices
    sections, ways, replicas = devices.shape
    fine = Mesh(devices.reshape(sections, ways // 2, 2, replicas), ("section", "z", "core", "dp"))
    tp = ("z", "core")
    in_specs = (
        P(tp, "dp"),
        P("dp", None, None),
        P("dp", None, None),
        P("section", tp),
        P("section", None, tp),
        P("section", None, None, tp),
        P("section", tp, None),
    )
    out_specs = (P("section", "dp", None, tp, None), P("section", "dp", None, tp, None))
    return jax.shard_map(shards, mesh=fine, in_specs=in_specs, out_specs=out_specs, check_vma=False)
```

```python
import functools

import jax
import jax.numpy as jnp
from jax import lax
from jax.experimental import pallas as pl
from jax.experimental.pallas import tpu as pltpu
from jax.sharding import Mesh
from jax.sharding import PartitionSpec as P

D = 8192
HD = 128
MICRO = 2
SEQ = 128
EPS = 1e-05
CHIPS = 8
SHARD = 512
HALF = SHARD // 2
STAT = 16
QROWS = 256
KVROWS = 256
OWN = QROWS + KVROWS // 2
KEEP = QROWS + KVROWS
SENT = QROWS + KVROWS
ROWS = 2 * OWN
ORDER = (0, -1, 1, -2, 2, -3, 3, 4)
BF = jnp.bfloat16
F32 = jnp.float32

FLIP, CORE, OTHER, WHICH = CHIPS, CHIPS + 1, CHIPS + 2, CHIPS + 3


def z_shift(value, hops):
    return lax.ppermute(value, "z", [(i, (i + hops) % CHIPS) for i in range(CHIPS)])


def sibling(value):
    return lax.ppermute(value, "core", [(0, 1), (1, 0)])


def along_section(value, hops):
    count = lax.axis_size("section")
    return lax.ppermute(value, "section", [(i, (i + hops) % count) for i in range(count)])


def diagonal(value, hops):
    count = lax.axis_size("section")
    pairs = [
        (s * CHIPS + i, ((s + 1) % count) * CHIPS + (i + hops) % CHIPS)
        for s in range(count)
        for i in range(CHIPS)
    ]
    return lax.ppermute(value, ("section", "z"), pairs)


def kv_route(value, step):
    pairs = []
    for a in range(2):
        for b in range(4):
            for c in range(2):
                z = 4 * a + b
                pairs.append((2 * z + c, 2 * (a + 2 * ((b + 2 * c + step) % 4)) + b // 2))
    return lax.ppermute(value, ("z", "core"), pairs)


def full(shape):
    return pl.BlockSpec(shape, lambda i, idx: (0,) * len(shape))


def call(body, indices, operands, specs, outs, flops=0):
    nbytes = sum(o.size * o.dtype.itemsize for o in outs)
    return pl.pallas_call(
        body,
        grid_spec=pltpu.PrefetchScalarGridSpec(
            num_scalar_prefetch=1,
            grid=(1,),
            in_specs=specs,
            out_specs=[full(o.shape) for o in outs],
        ),
        out_shape=outs,
        compiler_params=pltpu.CompilerParams(vmem_limit_bytes=24 * 2**20),
        cost_estimate=pl.CostEstimate(flops=flops, bytes_accessed=nbytes, transcendentals=0),
    )(indices, *operands)


def prepare_body(idx, x_ref, gain_ref, out_ref):
    x = x_ref[...].astype(F32)
    tokens = x.shape[1]
    for col in range(0, tokens, SEQ):
        out_ref[0:SHARD, col : col + SEQ] = (x[:, col : col + SEQ] * gain_ref[...]).astype(BF)
    total = jnp.sum(x * x, axis=0, keepdims=True)
    high = total.astype(BF)
    low = (total - high.astype(F32)).astype(BF)
    rows = lax.broadcasted_iota(jnp.int32, (STAT, tokens), 0)
    stat = jnp.where(rows == 0, high.astype(F32), jnp.where(rows == 1, low.astype(F32), 0.0))
    out_ref[SHARD : SHARD + STAT, :] = stat.astype(BF)


def prepare(idx, x, gain):
    tokens = x.shape[1]
    (out,) = call(
        prepare_body,
        idx,
        (x, gain),
        [full(x.shape), full(gain.shape)],
        [jax.ShapeDtypeStruct((SHARD + STAT, tokens), BF)],
        flops=4 * x.size,
    )
    return out


def stat_of(block):
    return block[0:1, :].astype(F32) + block[1:2, :].astype(F32)


def project_body(count, halves, first, final, idx, *refs):
    refs = list(refs)
    acc_refs = () if first else tuple(refs[:3])
    outs = refs[-2:] if final else refs[-3:]
    refs = refs[len(acc_refs) : -len(outs)]
    chunks, weights = refs[: count + halves], refs[count + halves :]
    own, other, stats = (None, None, None) if first else [ref[...] for ref in acc_refs]

    def add(total, part):
        return part if total is None else total + part

    for k in range(count):
        block = chunks[k][0:SHARD, :]
        own = add(own, jnp.dot(weights[2 * k][0], block, preferred_element_type=F32))
        other = add(other, jnp.dot(weights[2 * k + 1][0], block, preferred_element_type=F32))
        stat = stat_of(chunks[k][SHARD : SHARD + STAT, :])
        stats = add(stats, jnp.broadcast_to(stat, (8, stat.shape[1])))
    if halves:
        low, high = chunks[count], chunks[count + 1]
        block = jnp.concatenate([low[0:HALF, :], high[0:HALF, :]], axis=0)
        own = own + jnp.dot(weights[2 * count][0], block, preferred_element_type=F32)
        other = other + jnp.dot(weights[2 * count + 1][0], block, preferred_element_type=F32)
        stats = stats + jnp.broadcast_to(stat_of(high[HALF : HALF + STAT, :]), stats.shape)
    if final:
        keep_ref, send_ref = outs
        keep_ref[0:OWN, :] = own
        keep_ref[OWN:KEEP, :] = other[QROWS:OWN, :]
        keep_ref[KEEP : KEEP + 8, :] = stats
        send_ref[0 : OWN - QROWS, :] = own[QROWS:OWN, :]
        send_ref[OWN - QROWS : KVROWS, :] = other[QROWS:OWN, :]
        send_ref[KVROWS:SENT, :] = other[0:QROWS, :]
        send_ref[SENT : SENT + 8, :] = stats
    else:
        outs[0][...] = own
        outs[1][...] = other
        outs[2][...] = stats


def project(idx, acc, chunks, places, weights, halves=(), final=False):
    tokens = chunks[0].shape[1]
    arrays = list(chunks) + list(halves)
    operands = list(acc) + arrays
    specs = [full(a.shape) for a in operands]
    for place in places:
        for matrix in weights:
            specs.append(
                pl.BlockSpec((1, OWN, SHARD), lambda i, idx, place=place: (idx[place], 0, 0))
            )
            operands.append(matrix)
    rows = (KEEP + 8, SENT + 8) if final else (OWN, OWN, 8)
    return call(
        functools.partial(project_body, len(chunks), len(halves), not acc, final),
        idx,
        operands,
        specs,
        [jax.ShapeDtypeStruct((r, tokens), F32) for r in rows],
        flops=2 * ROWS * SHARD * tokens * len(places),
    )


def finish_body(idx, keep_ref, recv_ref, q_ref, kv_ref):
    mean = (keep_ref[KEEP : KEEP + 1, :] + recv_ref[SENT : SENT + 1, :]) * (1.0 / D)
    scale = lax.rsqrt(mean + EPS)
    q_ref[...] = ((keep_ref[0:QROWS, :] + recv_ref[KVROWS:SENT, :]) * scale).astype(BF)
    part = HD // 2
    own = (keep_ref[QROWS:OWN, :] + recv_ref[HD : 2 * HD, :]) * scale
    other = (keep_ref[OWN:KEEP, :] + recv_ref[0:HD, :]) * scale
    first = idx[CORE] == 0
    low, high = jnp.where(first, own, other).astype(BF), jnp.where(first, other, own).astype(BF)
    kv_ref[0:part, :] = low[0:part, :]
    kv_ref[part:HD, :] = high[0:part, :]
    kv_ref[HD : HD + part, :] = low[part:HD, :]
    kv_ref[HD + part : 2 * HD, :] = high[part:HD, :]


def finish(idx, keep, recv):
    tokens = keep.shape[1]
    return call(
        finish_body,
        idx,
        (keep, recv),
        [full(keep.shape), full(recv.shape)],
        [
            jax.ShapeDtypeStruct((QROWS, tokens), BF),
            jax.ShapeDtypeStruct((KVROWS, tokens), BF),
        ],
        flops=4 * 512 * tokens,
    )


def attend_body(idx, q_ref, first_ref, second_ref, mask_ref, out_ref):
    flip = idx[FLIP] == 1
    allowed = mask_ref[0] > 0.0
    one, two = first_ref[...], second_ref[...]
    for head in range(2):
        pair = jnp.where(flip, two, one) if head == 0 else jnp.where(flip, one, two)
        q = q_ref[head * HD : (head + 1) * HD, :]
        scores = lax.dot_general(
            pair[0:HD, :], q, (((0,), (0,)), ((), ())), preferred_element_type=F32
        ) * HD ** (-0.5)
        weights = jnp.where(allowed, jnp.exp(jnp.where(allowed, scores, 0.0)), 0.0)
        probs = (weights / jnp.sum(weights, axis=0, keepdims=True)).astype(BF)
        mixed = jnp.dot(pair[HD : 2 * HD, :], probs, preferred_element_type=F32)
        out_ref[head * HD : (head + 1) * HD, :] = mixed.astype(BF)


def attend(idx, q, first, second, mask):
    specs = [full(a.shape) for a in (q, first, second)]
    specs.append(pl.BlockSpec((1, SEQ, SEQ), lambda i, idx: (idx[WHICH], 0, 0)))
    (out,) = call(
        attend_body,
        idx,
        (q, first, second, mask),
        specs,
        [jax.ShapeDtypeStruct(q.shape, BF)],
        flops=8 * HD * SEQ * q.shape[1],
    )
    return out


def spread_body(kinds, idx, own_ref, other_ref, *refs):
    count = len(kinds)
    weights, outs = refs[: 2 * count], refs[2 * count :]
    own, other = own_ref[...], other_ref[...]
    for k in range(count):
        part = jnp.dot(weights[2 * k][0], own, preferred_element_type=F32)
        part = part + jnp.dot(weights[2 * k + 1][0], other, preferred_element_type=F32)
        outs[k][...] = part.astype(outs[k].dtype)


def spread(idx, own, other, places, kinds, weights):
    tokens = own.shape[1]
    specs = [full(own.shape), full(other.shape)]
    operands = [own, other]
    for place in places:
        for matrix in weights:
            specs.append(
                pl.BlockSpec((1, SHARD, QROWS), lambda i, idx, place=place: (idx[place], 0, 0))
            )
            operands.append(matrix)
    return call(
        functools.partial(spread_body, kinds),
        idx,
        operands,
        specs,
        [jax.ShapeDtypeStruct((SHARD, tokens), kind) for kind in kinds],
        flops=2 * SHARD * SHARD * tokens * len(places),
    )


def gather_project(idx, payload, w_in):
    right1, left1 = z_shift(payload, 1), z_shift(payload, -1)
    acc = project(idx, (), [payload], [0], w_in)
    right2, left2 = z_shift(right1, 1), z_shift(left1, -1)
    acc = project(idx, acc, [right1, left1], [1, 2], w_in)
    right3, left3 = z_shift(right2, 1), z_shift(left2, -1)
    right4, left4 = z_shift(right2[:HALF], 2), z_shift(left2[HALF:], -2)
    acc = project(idx, acc, [right2, left2], [3, 4], w_in)
    return project(idx, acc, [right3, left3], [5, 6, 7], w_in, (right4, left4), final=True)


def layer(idx, x, payload, mask, w_in, w_out, last):
    keep, send = gather_project(idx, payload, w_in)
    q, kv = finish(idx, keep, sibling(send))
    first, second = kv_route(kv, 0), kv_route(kv, 1)
    mixed = attend(idx, q, first, second, mask)
    other = sibling(mixed)
    far_left, far_right, opposite = spread(idx, mixed, other, [5, 6, 7], (BF,) * 3, w_out)
    to_right, to_left = z_shift(far_right, 1), z_shift(far_left, -1)
    low, high = z_shift(opposite[:HALF], 2), z_shift(opposite[HALF:], -2)
    two_left, two_right, one_left, one_right, own = spread(
        idx, mixed, other, [3, 4, 1, 2, 0], (F32,) * 5, w_out
    )
    base = x.astype(F32) + own
    zeros = jnp.zeros_like(low)
    to_right = (
        two_right + to_right.astype(F32) + jnp.concatenate([low, zeros], 0).astype(F32)
    ).astype(BF)
    to_left = (
        two_left + to_left.astype(F32) + jnp.concatenate([zeros, high], 0).astype(F32)
    ).astype(BF)
    if not last:
        base = along_section(base.astype(BF), 1).astype(F32)
    to_right, to_left = z_shift(to_right, 1), z_shift(to_left, -1)
    to_right = (one_right + to_right.astype(F32)).astype(BF)
    to_left = (one_left + to_left.astype(F32)).astype(BF)
    move = z_shift if last else diagonal
    to_right, to_left = move(to_right, 1), move(to_left, -1)
    return (base + to_right.astype(F32) + to_left.astype(F32)).astype(BF)


def pack(rollout, source):
    tokens = rollout.shape[1]
    place = lax.axis_index("dp")
    count = lax.axis_size("dp")
    blocks = [rollout]
    for hops in range(1, count):
        pairs = [(i, (i + hops) % count) for i in range(count)]
        blocks.append(lax.ppermute(rollout, "dp", pairs))
    ids = jnp.concatenate(
        [
            (place - hops) % count * tokens + jnp.arange(tokens, dtype=jnp.int32)
            for hops in range(count)
        ]
    )
    chosen = (ids[:, None] == source[None, :]).astype(BF)
    return jnp.dot(
        jnp.concatenate(blocks, axis=1), chosen, preferred_element_type=F32
    ).astype(BF)


def split_in_body(idx, q_own, q_other, kv_own, kv_other, own_ref, send_ref):
    half = HD // 2
    for q_ref, kv_ref, out_ref in ((q_own, kv_own, own_ref), (q_other, kv_other, send_ref)):
        out_ref[0, 0:QROWS, :] = q_ref[...].T
        out_ref[0, QROWS : QROWS + half, :] = kv_ref[0]
        out_ref[0, QROWS + half : OWN, :] = kv_ref[1]


def split_out_body(idx, own_in, other_in, own_ref, send_ref):
    own_ref[0] = own_in[...].T
    send_ref[0] = other_in[...].T


def split(body, idx, operands, specs, rows, cols):
    shape = jax.ShapeDtypeStruct((CHIPS, rows, cols), BF)
    own, send = pl.pallas_call(
        body,
        grid_spec=pltpu.PrefetchScalarGridSpec(
            num_scalar_prefetch=1,
            grid=(CHIPS,),
            in_specs=specs,
            out_specs=[pl.BlockSpec((1, rows, cols), lambda i, idx: (i, 0, 0))] * 2,
        ),
        out_shape=[shape, shape],
        compiler_params=pltpu.CompilerParams(vmem_limit_bytes=24 * 2**20),
        cost_estimate=pl.CostEstimate(
            flops=0, bytes_accessed=8 * CHIPS * rows * cols, transcendentals=0
        ),
    )(idx, *operands)
    return own, sibling(send)


def weights_in(idx, wq, wkv):
    kv = wkv.transpose(0, 2, 1)
    q_spec = lambda at: pl.BlockSpec((SHARD, QROWS), lambda i, idx: (2 * i + idx[at], 0))
    kv_spec = lambda at: pl.BlockSpec((2, HD // 2, SHARD), lambda i, idx: (0, 0, 2 * i + idx[at]))
    specs = [q_spec(CORE), q_spec(OTHER), kv_spec(CORE), kv_spec(OTHER)]
    return split(split_in_body, idx, (wq, wq, kv, kv), specs, OWN, SHARD)


def weights_out(idx, wo):
    spec = lambda at: pl.BlockSpec((QROWS, SHARD), lambda i, idx: (0, 2 * i + idx[at]))
    return split(split_out_body, idx, (wo, wo), [spec(CORE), spec(OTHER)], SHARD, QROWS)


def shards(rollout_acts, pack_source, segments, gain, wq, wkv, wo):
    section = lax.axis_index("section")
    count = lax.axis_size("section")
    z, core = lax.axis_index("z"), lax.axis_index("core")
    places = [(z + k) % CHIPS for k in ORDER] + [(z // 2) % 2, core, 1 - core]

    def index(clock):
        return jnp.stack(places + [jnp.clip(clock - section, 0, MICRO - 1)]).astype(jnp.int32)

    packed = pack(rollout_acts, pack_source[0].reshape(-1))
    packed = [packed[:, m * SEQ : (m + 1) * SEQ] for m in range(MICRO)]
    w_in = weights_in(index(0), wq[0], wkv[0])
    gains = jnp.broadcast_to(gain[0].astype(F32)[:, None], (SHARD, SEQ))
    seg = segments[0]
    spots = jnp.arange(SEQ, dtype=jnp.int32)
    mask = (
        (seg[:, :, None] == seg[:, None, :]) & (spots[:, None] <= spots[None, :])[None]
    ).astype(F32)
    taken = list(packed)
    clocks = MICRO + count - 1
    mirror = lambda v: lax.ppermute(v, "section", [(i, count - 1 - i) for i in range(count)])
    x = packed[0]
    for clock in range(clocks):
        if 0 < clock < MICRO:
            x = jnp.where(section == 0, packed[clock], x)
        for m in range(MICRO):
            if m < clock < m + count:
                taken[m] = jnp.where(section == clock - m, x, taken[m])
        last = clock == clocks - 1
        if last:
            mirrored = [mirror(v) for v in taken]
            done = [jnp.where(section == 0, x, taken[0]), taken[1]]
            produced = [along_section(v, -1) for v in done]
        idx = index(clock)
        payload = prepare(idx, x, gains)
        if clock == 0:
            wo, payload = lax.optimization_barrier((wo, payload))
            w_out = weights_out(idx, wo[0])
        x = layer(idx, x, payload, mask, w_in, w_out, last)
    produced[1] = jnp.where(section == count - 1, x, produced[1])
    return (jnp.stack(produced)[None, None], jnp.stack(mirrored)[None, None])


def solution(mesh):
    devices = mesh.devices
    sections, ways, replicas = devices.shape
    fine = Mesh(devices.reshape(sections, ways // 2, 2, replicas), ("section", "z", "core", "dp"))
    tp = ("z", "core")
    in_specs = (
        P(tp, "dp"),
        P("dp", None, None),
        P("dp", None, None),
        P("section", tp),
        P("section", None, tp),
        P("section", None, None, tp),
        P("section", tp, None),
    )
    out_specs = (P("section", "dp", None, tp, None), P("section", "dp", None, tp, None))
    return jax.shard_map(shards, mesh=fine, in_specs=in_specs, out_specs=out_specs, check_vma=False)
```

```python
import functools

import jax
import jax.numpy as jnp
from jax import lax
from jax.experimental import pallas as pl
from jax.experimental.pallas import tpu as pltpu
from jax.sharding import Mesh
from jax.sharding import PartitionSpec as P

D = 8192
HD = 128
MICRO = 2
SEQ = 128
EPS = 1e-05
CHIPS = 8
SHARD = 512
HALF = SHARD // 2
STAT = 16
QROWS = 256
KVROWS = 256
OWN = QROWS + KVROWS // 2
KEEP = QROWS + KVROWS
SENT = QROWS + KVROWS
ROWS = 2 * OWN
ORDER = (0, -1, 1, -2, 2, -3, 3, 4)
BF = jnp.bfloat16
F32 = jnp.float32

FLIP, CORE, OTHER, WHICH = CHIPS, CHIPS + 1, CHIPS + 2, CHIPS + 3
TURN_LIMIT = 8


def z_shift(value, hops):
    return lax.ppermute(value, "z", [(i, (i + hops) % CHIPS) for i in range(CHIPS)])


def sibling(value):
    return lax.ppermute(value, "core", [(0, 1), (1, 0)])


def along_section(value, hops):
    count = lax.axis_size("section")
    return lax.ppermute(value, "section", [(i, (i + hops) % count) for i in range(count)])


def diagonal(value, hops):
    count = lax.axis_size("section")
    pairs = [
        (s * CHIPS + i, ((s + 1) % count) * CHIPS + (i + hops) % CHIPS)
        for s in range(count)
        for i in range(CHIPS)
    ]
    return lax.ppermute(value, ("section", "z"), pairs)


def kv_route(value, step):
    pairs = []
    for a in range(2):
        for b in range(4):
            for c in range(2):
                z = 4 * a + b
                pairs.append((2 * z + c, 2 * (a + 2 * ((b + 2 * c + step) % 4)) + b // 2))
    return lax.ppermute(value, ("z", "core"), pairs)


def call(body, indices, operands, outs, flops=0):
    nbytes = sum(o.size * o.dtype.itemsize for o in outs)
    return pl.pallas_call(
        body,
        in_specs=[pl.BlockSpec(memory_space=pltpu.SMEM)]
        + [pl.BlockSpec(memory_space=pltpu.VMEM)] * len(operands),
        out_specs=[pl.BlockSpec(memory_space=pltpu.VMEM)] * len(outs),
        out_shape=outs,
        compiler_params=pltpu.CompilerParams(vmem_limit_bytes=8 * 2**20),
        cost_estimate=pl.CostEstimate(flops=flops, bytes_accessed=nbytes, transcendentals=0),
    )(indices, *operands)


def write_payload(x, gain_ref, out_ref):
    tokens = x.shape[1]
    out_ref[0:SHARD, :] = (x * gain_ref[...]).astype(BF)
    total = jnp.sum(x * x, axis=0, keepdims=True)
    high = total.astype(BF)
    low = (total - high.astype(F32)).astype(BF)
    rows = lax.broadcasted_iota(jnp.int32, (STAT, tokens), 0)
    stat = jnp.where(rows == 0, high.astype(F32), jnp.where(rows == 1, low.astype(F32), 0.0))
    out_ref[SHARD : SHARD + STAT, :] = stat.astype(BF)


def prepare_body(idx, x_ref, gain_ref, out_ref):
    write_payload(x_ref[...].astype(F32), gain_ref, out_ref)


def prepare(idx, x, gain):
    shape = jax.ShapeDtypeStruct((SHARD + STAT, x.shape[1]), BF)
    (out,) = call(prepare_body, idx, (x, gain), [shape], flops=4 * x.size)
    return out


def combine_body(idx, base_ref, right_ref, left_ref, gain_ref, x_ref, out_ref):
    total = base_ref[...].astype(F32) + right_ref[...].astype(F32) + left_ref[...].astype(F32)
    x_ref[...] = total.astype(BF)
    write_payload(x_ref[...].astype(F32), gain_ref, out_ref)


def combine(idx, base, right, left, gain):
    shapes = [
        jax.ShapeDtypeStruct(right.shape, BF),
        jax.ShapeDtypeStruct((SHARD + STAT, right.shape[1]), BF),
    ]
    return call(combine_body, idx, (base, right, left, gain), shapes, flops=8 * right.size)


def stat_of(block):
    return block[0:1, :].astype(F32) + block[1:2, :].astype(F32)


def project_body(places, count, halves, first, final, idx, *refs):
    acc_refs = () if first else refs[:2]
    outs = refs[-2:]
    chunks, weights = refs[len(acc_refs) : -3], refs[-3]
    total, stats = (None, None) if first else [ref[...] for ref in acc_refs]

    def add(value, part):
        return part if value is None else value + part

    blocks = [(ref[0:SHARD, :], stat_of(ref[SHARD : SHARD + STAT, :])) for ref in chunks[:count]]
    if halves:
        low, high = chunks[count], chunks[count + 1]
        block = jnp.concatenate([low[0:HALF, :], high[0:HALF, :]], axis=0)
        blocks.append((block, stat_of(high[HALF : HALF + STAT, :])))
    for place, (block, stat) in zip(places, blocks):
        total = add(total, jnp.dot(weights[idx[place]], block, preferred_element_type=F32))
        stats = add(stats, jnp.broadcast_to(stat, (8, stat.shape[1])))
    if final:
        keep_ref, send_ref = outs
        keep_ref[0:OWN, :] = total[0:OWN, :]
        keep_ref[OWN:KEEP, :] = total[OWN + QROWS : ROWS, :]
        keep_ref[KEEP : KEEP + 8, :] = stats
        send_ref[0 : OWN - QROWS, :] = total[QROWS:OWN, :]
        send_ref[OWN - QROWS : KVROWS, :] = total[OWN + QROWS : ROWS, :]
        send_ref[KVROWS:SENT, :] = total[OWN : OWN + QROWS, :]
        send_ref[SENT : SENT + 8, :] = stats
    else:
        outs[0][...] = total
        outs[1][...] = stats


def project(idx, acc, chunks, places, weights, halves=(), final=False):
    tokens = chunks[0].shape[1]
    operands = [*acc, *chunks, *halves, weights]
    rows = (KEEP + 8, SENT + 8) if final else (ROWS, 8)
    return call(
        functools.partial(project_body, places, len(chunks), len(halves), not acc, final),
        idx,
        operands,
        [jax.ShapeDtypeStruct((r, tokens), F32) for r in rows],
        flops=2 * ROWS * SHARD * tokens * len(places),
    )


def finish_body(idx, keep_ref, recv_ref, q_ref, kv_ref):
    mean = (keep_ref[KEEP : KEEP + 1, :] + recv_ref[SENT : SENT + 1, :]) * (1.0 / D)
    scale = lax.rsqrt(mean + EPS)
    q_ref[...] = ((keep_ref[0:QROWS, :] + recv_ref[KVROWS:SENT, :]) * scale).astype(BF)
    part = HD // 2
    own = (keep_ref[QROWS:OWN, :] + recv_ref[HD : 2 * HD, :]) * scale
    other = (keep_ref[OWN:KEEP, :] + recv_ref[0:HD, :]) * scale
    first = idx[CORE] == 0
    low, high = jnp.where(first, own, other).astype(BF), jnp.where(first, other, own).astype(BF)
    kv_ref[0:part, :] = low[0:part, :]
    kv_ref[part:HD, :] = high[0:part, :]
    kv_ref[HD : HD + part, :] = low[part:HD, :]
    kv_ref[HD + part : 2 * HD, :] = high[part:HD, :]


def finish(idx, keep, recv):
    tokens = keep.shape[1]
    return call(
        finish_body,
        idx,
        (keep, recv),
        [
            jax.ShapeDtypeStruct((QROWS, tokens), BF),
            jax.ShapeDtypeStruct((KVROWS, tokens), BF),
        ],
        flops=4 * 512 * tokens,
    )


def attend_body(idx, q_ref, first_ref, second_ref, mask_ref, out_ref):
    flip = idx[FLIP] == 1
    allowed = mask_ref[idx[WHICH]] > 0.0
    one, two = first_ref[...], second_ref[...]
    for head in range(2):
        pair = jnp.where(flip, two, one) if head == 0 else jnp.where(flip, one, two)
        q = q_ref[head * HD : (head + 1) * HD, :]
        scores = lax.dot_general(
            pair[0:HD, :], q, (((0,), (0,)), ((), ())), preferred_element_type=F32
        ) * HD ** (-0.5)
        weights = jnp.where(allowed, jnp.exp(jnp.where(allowed, scores, 0.0)), 0.0)
        probs = (weights / jnp.sum(weights, axis=0, keepdims=True)).astype(BF)
        mixed = jnp.dot(pair[HD : 2 * HD, :], probs, preferred_element_type=F32)
        out_ref[head * HD : (head + 1) * HD, :] = mixed.astype(BF)


def attend(idx, q, first, second, mask):
    (out,) = call(
        attend_body,
        idx,
        (q, first, second, mask),
        [jax.ShapeDtypeStruct(q.shape, BF)],
        flops=8 * HD * SEQ * q.shape[1],
    )
    return out


def spread_body(places, idx, heads_ref, other_heads_ref, weights, *outs):
    heads = jnp.concatenate([heads_ref[...], other_heads_ref[...]], axis=0)
    for place, out_ref in zip(places, outs):
        part = jnp.dot(weights[idx[place]], heads, preferred_element_type=F32)
        out_ref[...] = part.astype(out_ref.dtype)


def spread(idx, own, other, places, kind, weights):
    tokens = own.shape[1]
    return call(
        functools.partial(spread_body, places),
        idx,
        (own, other, weights),
        [jax.ShapeDtypeStruct((SHARD, tokens), kind) for _ in places],
        flops=2 * SHARD * SHARD * tokens * len(places),
    )


def tied(first, second):
    return lax.optimization_barrier((first, second))


def gather_project(idx, payload, w_in):
    one = (z_shift(payload, 1), z_shift(payload, -1))
    acc = project(idx, (), [payload], [0], w_in)
    one, acc = tied(one, acc)
    two = (z_shift(one[0], 1), z_shift(one[1], -1))
    acc = project(idx, acc, one, [1, 2], w_in)
    two, acc = tied(two, acc)
    three = (z_shift(two[0], 1), z_shift(two[1], -1))
    halves = (z_shift(two[0][:HALF], 2), z_shift(two[1][HALF:], -2))
    acc = project(idx, acc, two, [3, 4], w_in)
    (three, halves), acc = tied((three, halves), acc)
    return project(idx, acc, three, [5, 6, 7], w_in, halves, final=True)


def layer(idx, x, payload, mask, w_in, w_out, last):
    keep, send = gather_project(idx, payload, w_in)
    q, kv = finish(idx, keep, sibling(send))
    first, second = kv_route(kv, 0), kv_route(kv, 1)
    mixed = attend(idx, q, first, second, mask)
    other = sibling(mixed)
    far_left, far_right, opposite = spread(idx, mixed, other, [5, 6, 7], BF, w_out)
    sent = (z_shift(far_right, 1), z_shift(far_left, -1))
    halves = (z_shift(opposite[:HALF], 2), z_shift(opposite[HALF:], -2))
    parts = spread(idx, mixed, other, [3, 4, 1, 2, 0], F32, w_out)
    (sent, halves), parts = tied((sent, halves), parts)
    two_left, two_right, one_left, one_right, own = parts
    base = x.astype(F32) + own
    zeros = jnp.zeros_like(halves[0])
    low, high = jnp.concatenate([halves[0], zeros], 0), jnp.concatenate([zeros, halves[1]], 0)
    to_right = (two_right + sent[0].astype(F32) + low.astype(F32)).astype(BF)
    to_left = (two_left + sent[1].astype(F32) + high.astype(F32)).astype(BF)
    if not last:
        base = along_section(base.astype(BF), 1)
    to_right, to_left = z_shift(to_right, 1), z_shift(to_left, -1)
    to_right = (one_right + to_right.astype(F32)).astype(BF)
    to_left = (one_left + to_left.astype(F32)).astype(BF)
    move = z_shift if last else diagonal
    return base, move(to_right, 1), move(to_left, -1)


def pack(rollout, source):
    tokens = rollout.shape[1]
    place = lax.axis_index("dp")
    count = lax.axis_size("dp")
    blocks = [rollout]
    for hops in range(1, count):
        pairs = [(i, (i + hops) % count) for i in range(count)]
        blocks.append(lax.ppermute(rollout, "dp", pairs))
    ids = jnp.concatenate(
        [
            (place - hops) % count * tokens + jnp.arange(tokens, dtype=jnp.int32)
            for hops in range(count)
        ]
    )
    chosen = (ids[:, None] == source[None, :]).astype(BF)
    return jnp.dot(
        jnp.concatenate(blocks, axis=1), chosen, preferred_element_type=F32
    ).astype(BF)


def turn_in_body(idx, q_ref, kv_ref, other_q_ref, other_kv_ref, out_ref):
    half = HD // 2
    for base, q, kv in ((0, q_ref, kv_ref), (OWN, other_q_ref, other_kv_ref)):
        out_ref[0, base : base + QROWS, :] = q[...].T
        out_ref[0, base + QROWS : base + QROWS + half, :] = kv[0]
        out_ref[0, base + QROWS + half : base + OWN, :] = kv[1]


def turn_out_body(idx, own_ref, other_ref, out_ref):
    out_ref[0, :, 0:QROWS] = own_ref[...].T
    out_ref[0, :, QROWS:SHARD] = other_ref[...].T


def turn(body, idx, operands, specs, rows, cols):
    return pl.pallas_call(
        body,
        grid_spec=pltpu.PrefetchScalarGridSpec(
            num_scalar_prefetch=1,
            grid=(CHIPS,),
            in_specs=specs,
            out_specs=pl.BlockSpec((1, rows, cols), lambda i, idx: (i, 0, 0)),
        ),
        out_shape=jax.ShapeDtypeStruct((CHIPS, rows, cols), BF),
        compiler_params=pltpu.CompilerParams(vmem_limit_bytes=TURN_LIMIT * 2**20),
        cost_estimate=pl.CostEstimate(
            flops=0, bytes_accessed=4 * CHIPS * rows * cols, transcendentals=0
        ),
    )(idx, *operands)


def turn_in(idx, own, other):
    specs = [
        pl.BlockSpec((SHARD, QROWS), lambda i, idx: (2 * i + idx[CORE], 0)),
        pl.BlockSpec((2, HD // 2, SHARD), lambda i, idx: (0, 0, 2 * i + idx[CORE])),
    ]
    return turn(turn_in_body, idx, (*own, *other), specs * 2, ROWS, SHARD)


def turn_out(idx, own, other):
    spec = pl.BlockSpec((QROWS, SHARD), lambda i, idx: (0, 2 * i + idx[CORE]))
    return turn(turn_out_body, idx, (own, other), [spec] * 2, SHARD, SHARD)


def shards(rollout_acts, pack_source, segments, gain, wq, wkv, wo):
    section = lax.axis_index("section")
    count = lax.axis_size("section")
    z, core = lax.axis_index("z"), lax.axis_index("core")
    order = (z + jnp.array(ORDER, jnp.int32)) & (CHIPS - 1)

    def index(clock):
        rest = [(z >> 1) & 1, core, 1 - core, jnp.clip(clock - section, 0, MICRO - 1)]
        return jnp.concatenate([order, jnp.stack(rest)]).astype(jnp.int32)

    wq, wkv, wo = wq[0], wkv[0].transpose(0, 2, 1), wo[0]
    wq_other, wkv_other = sibling(wq), sibling(wkv)
    packed = pack(rollout_acts, pack_source[0].reshape(-1))
    packed = [packed[:, m * SEQ : (m + 1) * SEQ] for m in range(MICRO)]
    gains = jnp.broadcast_to(gain[0].astype(F32)[:, None], (SHARD, SEQ))
    seg = segments[0]
    spots = jnp.arange(SEQ, dtype=jnp.int32)
    mask = (
        (seg[:, :, None] == seg[:, None, :]) & (spots[:, None] <= spots[None, :])[None]
    ).astype(F32)
    taken = list(packed)
    clocks = MICRO + count - 1
    mirror = lambda v: lax.ppermute(v, "section", [(i, count - 1 - i) for i in range(count)])
    x = packed[0]
    payload = prepare(index(0), x, gains)
    (wo, wq_other, wkv_other), payload = tied((wo, wq_other, wkv_other), payload)
    w_in = turn_in(index(0), (wq, wkv), (wq_other, wkv_other))
    w_out = turn_out(index(0), wo, sibling(wo))
    for clock in range(clocks):
        for m in range(MICRO):
            if m < clock < m + count:
                taken[m] = jnp.where(section == clock - m, x, taken[m])
        last = clock == clocks - 1
        if last:
            mirrored = [mirror(v) for v in taken]
            done = [jnp.where(section == 0, x, taken[0]), taken[1]]
            produced = [along_section(v, -1) for v in done]
        idx = index(clock)
        terms = layer(idx, x, payload, mask, w_in, w_out, last)
        if last or clock + 1 < MICRO:
            x = sum(term.astype(F32) for term in terms).astype(BF)
            if not last:
                x = jnp.where(section == 0, packed[clock + 1], x)
                payload = prepare(idx, x, gains)
        else:
            x, payload = combine(idx, *terms, gains)
    produced[1] = jnp.where(section == count - 1, x, produced[1])
    return (jnp.stack(produced)[None, None], jnp.stack(mirrored)[None, None])


def solution(mesh):
    devices = mesh.devices
    sections, ways, replicas = devices.shape
    fine = Mesh(devices.reshape(sections, ways // 2, 2, replicas), ("section", "z", "core", "dp"))
    tp = ("z", "core")
    in_specs = (
        P(tp, "dp"),
        P("dp", None, None),
        P("dp", None, None),
        P("section", tp),
        P("section", None, tp),
        P("section", None, None, tp),
        P("section", tp, None),
    )
    out_specs = (P("section", "dp", None, tp, None), P("section", "dp", None, tp, None))
    return jax.shard_map(shards, mesh=fine, in_specs=in_specs, out_specs=out_specs, check_vma=False)
```

```python
import functools

import jax
import jax.numpy as jnp
from jax import lax
from jax.experimental import pallas as pl
from jax.experimental.pallas import tpu as pltpu
from jax.sharding import Mesh
from jax.sharding import PartitionSpec as P

D = 8192
HD = 128
MICRO = 2
SEQ = 128
EPS = 1e-05
CHIPS = 8
SHARD = 512
HALF = SHARD // 2
STAT = 16
QROWS = 256
KVROWS = 256
OWN = QROWS + KVROWS // 2
KEEP = QROWS + KVROWS
SENT = QROWS + KVROWS
ROWS = 2 * OWN
ORDER = (0, -1, 1, -2, 2, -3, 3, 4)
BF = jnp.bfloat16
F32 = jnp.float32

FLIP, CORE, OTHER, WHICH = CHIPS, CHIPS + 1, CHIPS + 2, CHIPS + 3
TURN_LIMIT = 8


def z_shift(value, hops):
    return lax.ppermute(value, "z", [(i, (i + hops) % CHIPS) for i in range(CHIPS)])


def sibling(value):
    return lax.ppermute(value, "core", [(0, 1), (1, 0)])


def along_section(value, hops):
    count = lax.axis_size("section")
    return lax.ppermute(value, "section", [(i, (i + hops) % count) for i in range(count)])


def diagonal(value, hops):
    count = lax.axis_size("section")
    pairs = [
        (s * CHIPS + i, ((s + 1) % count) * CHIPS + (i + hops) % CHIPS)
        for s in range(count)
        for i in range(CHIPS)
    ]
    return lax.ppermute(value, ("section", "z"), pairs)


def kv_route(value, step):
    pairs = []
    for a in range(2):
        for b in range(4):
            for c in range(2):
                z = 4 * a + b
                pairs.append((2 * z + c, 2 * (a + 2 * ((b + 2 * c + step) % 4)) + b // 2))
    return lax.ppermute(value, ("z", "core"), pairs)


def call(body, indices, operands, outs, flops=0):
    nbytes = sum(o.size * o.dtype.itemsize for o in outs)
    return pl.pallas_call(
        body,
        in_specs=[pl.BlockSpec(memory_space=pltpu.SMEM)]
        + [pl.BlockSpec(memory_space=pltpu.VMEM)] * len(operands),
        out_specs=[pl.BlockSpec(memory_space=pltpu.VMEM)] * len(outs),
        out_shape=outs,
        compiler_params=pltpu.CompilerParams(vmem_limit_bytes=8 * 2**20),
        cost_estimate=pl.CostEstimate(flops=flops, bytes_accessed=nbytes, transcendentals=0),
    )(indices, *operands)


def write_payload(x, gain_ref, out_ref):
    tokens = x.shape[1]
    out_ref[0:SHARD, :] = (x * gain_ref[...]).astype(BF)
    total = jnp.sum(x * x, axis=0, keepdims=True)
    high = total.astype(BF)
    low = (total - high.astype(F32)).astype(BF)
    rows = lax.broadcasted_iota(jnp.int32, (STAT, tokens), 0)
    stat = jnp.where(rows == 0, high.astype(F32), jnp.where(rows == 1, low.astype(F32), 0.0))
    out_ref[SHARD : SHARD + STAT, :] = stat.astype(BF)


def prepare_body(idx, x_ref, gain_ref, out_ref):
    write_payload(x_ref[...].astype(F32), gain_ref, out_ref)


def prepare(idx, x, gain):
    shape = jax.ShapeDtypeStruct((SHARD + STAT, x.shape[1]), BF)
    (out,) = call(prepare_body, idx, (x, gain), [shape], flops=4 * x.size)
    return out


def combine_body(idx, base_ref, right_ref, left_ref, gain_ref, x_ref, out_ref):
    total = base_ref[...].astype(F32) + right_ref[...].astype(F32) + left_ref[...].astype(F32)
    x_ref[...] = total.astype(BF)
    write_payload(x_ref[...].astype(F32), gain_ref, out_ref)


def combine(idx, base, right, left, gain):
    shapes = [
        jax.ShapeDtypeStruct(right.shape, BF),
        jax.ShapeDtypeStruct((SHARD + STAT, right.shape[1]), BF),
    ]
    return call(combine_body, idx, (base, right, left, gain), shapes, flops=8 * right.size)


def stat_of(block):
    return block[0:1, :].astype(F32) + block[1:2, :].astype(F32)


def project_body(places, first, final, idx, *refs):
    acc_refs = () if first else refs[:2]
    outs = refs[-2:]
    chunks, weights = refs[len(acc_refs) : -3], refs[-3]
    total, stats = (None, None) if first else [ref[...] for ref in acc_refs]

    def add(value, part):
        return part if value is None else value + part

    blocks = [(ref[0:SHARD, :], stat_of(ref[SHARD : SHARD + STAT, :])) for ref in chunks]
    for place, (block, stat) in zip(places, blocks):
        total = add(total, jnp.dot(weights[idx[place]], block, preferred_element_type=F32))
        stats = add(stats, jnp.broadcast_to(stat, (8, stat.shape[1])))
    if final:
        keep_ref, send_ref = outs
        keep_ref[0:OWN, :] = total[0:OWN, :]
        keep_ref[OWN:KEEP, :] = total[OWN + QROWS : ROWS, :]
        keep_ref[KEEP : KEEP + 8, :] = stats
        send_ref[0 : OWN - QROWS, :] = total[QROWS:OWN, :]
        send_ref[OWN - QROWS : KVROWS, :] = total[OWN + QROWS : ROWS, :]
        send_ref[KVROWS:SENT, :] = total[OWN : OWN + QROWS, :]
        send_ref[SENT : SENT + 8, :] = stats
    else:
        outs[0][...] = total
        outs[1][...] = stats


def project(idx, acc, chunks, places, weights, final=False):
    tokens = chunks[0].shape[1]
    operands = [*acc, *chunks, weights]
    rows = (KEEP + 8, SENT + 8) if final else (ROWS, 8)
    return call(
        functools.partial(project_body, places, not acc, final),
        idx,
        operands,
        [jax.ShapeDtypeStruct((r, tokens), F32) for r in rows],
        flops=2 * ROWS * SHARD * tokens * len(places),
    )


def finish_body(idx, keep_ref, recv_ref, q_ref, kv_ref):
    mean = (keep_ref[KEEP : KEEP + 1, :] + recv_ref[SENT : SENT + 1, :]) * (1.0 / D)
    scale = lax.rsqrt(mean + EPS)
    q_ref[...] = ((keep_ref[0:QROWS, :] + recv_ref[KVROWS:SENT, :]) * scale).astype(BF)
    part = HD // 2
    own = (keep_ref[QROWS:OWN, :] + recv_ref[HD : 2 * HD, :]) * scale
    other = (keep_ref[OWN:KEEP, :] + recv_ref[0:HD, :]) * scale
    first = idx[CORE] == 0
    low, high = jnp.where(first, own, other).astype(BF), jnp.where(first, other, own).astype(BF)
    kv_ref[0:part, :] = low[0:part, :]
    kv_ref[part:HD, :] = high[0:part, :]
    kv_ref[HD : HD + part, :] = low[part:HD, :]
    kv_ref[HD + part : 2 * HD, :] = high[part:HD, :]


def finish(idx, keep, recv):
    tokens = keep.shape[1]
    return call(
        finish_body,
        idx,
        (keep, recv),
        [
            jax.ShapeDtypeStruct((QROWS, tokens), BF),
            jax.ShapeDtypeStruct((KVROWS, tokens), BF),
        ],
        flops=4 * 512 * tokens,
    )


def attend_body(idx, q_ref, first_ref, second_ref, mask_ref, out_ref):
    flip = idx[FLIP] == 1
    allowed = mask_ref[idx[WHICH]] > 0.0
    one, two = first_ref[...], second_ref[...]
    for head in range(2):
        pair = jnp.where(flip, two, one) if head == 0 else jnp.where(flip, one, two)
        q = q_ref[head * HD : (head + 1) * HD, :]
        scores = lax.dot_general(
            pair[0:HD, :], q, (((0,), (0,)), ((), ())), preferred_element_type=F32
        ) * HD ** (-0.5)
        weights = jnp.where(allowed, jnp.exp(jnp.where(allowed, scores, 0.0)), 0.0)
        probs = (weights / jnp.sum(weights, axis=0, keepdims=True)).astype(BF)
        mixed = jnp.dot(pair[HD : 2 * HD, :], probs, preferred_element_type=F32)
        out_ref[head * HD : (head + 1) * HD, :] = mixed.astype(BF)


def attend(idx, q, first, second, mask):
    (out,) = call(
        attend_body,
        idx,
        (q, first, second, mask),
        [jax.ShapeDtypeStruct(q.shape, BF)],
        flops=8 * HD * SEQ * q.shape[1],
    )
    return out


def spread_body(places, idx, heads_ref, other_heads_ref, weights, *outs):
    heads = jnp.concatenate([heads_ref[...], other_heads_ref[...]], axis=0)
    for place, out_ref in zip(places, outs):
        part = jnp.dot(weights[idx[place]], heads, preferred_element_type=F32)
        out_ref[...] = part.astype(out_ref.dtype)


def spread(idx, own, other, places, kinds, weights):
    tokens = own.shape[1]
    return call(
        functools.partial(spread_body, places),
        idx,
        (own, other, weights),
        [jax.ShapeDtypeStruct((SHARD, tokens), kind) for kind in kinds],
        flops=2 * SHARD * SHARD * tokens * len(places),
    )


def tied(first, second):
    return lax.optimization_barrier((first, second))


def gather_project(idx, payload, w_in):
    one = (z_shift(payload, 1), z_shift(payload, -1))
    opposite = z_shift(payload, CHIPS // 2)
    acc = project(idx, (), [payload], [0], w_in)
    one, acc = tied(one, acc)
    two = (z_shift(one[0], 1), z_shift(one[1], -1))
    acc = project(idx, acc, one, [1, 2], w_in)
    (two, opposite), acc = tied((two, opposite), acc)
    three = (z_shift(two[0], 1), z_shift(two[1], -1))
    acc = project(idx, acc, [*two, opposite], [3, 4, 7], w_in)
    three, acc = tied(three, acc)
    return project(idx, acc, three, [5, 6], w_in, final=True)


def layer(idx, x, payload, mask, w_in, w_out, last):
    keep, send = gather_project(idx, payload, w_in)
    q, kv = finish(idx, keep, sibling(send))
    first, second = kv_route(kv, 0), kv_route(kv, 1)
    mixed = attend(idx, q, first, second, mask)
    other = sibling(mixed)
    *far, own = spread(idx, mixed, other, [5, 6, 7, 0], (BF, BF, BF, F32), w_out)
    far_left, far_right, opposite = far
    sent = (z_shift(far_right, 1), z_shift(far_left, -1))
    halves = (z_shift(opposite[:HALF], 2), z_shift(opposite[HALF:], -2))
    base = x.astype(F32) + own
    if not last:
        base = along_section(base.astype(BF), 1)
    parts = spread(idx, mixed, other, [3, 4, 1, 2], (F32,) * 4, w_out)
    (sent, halves, base), parts = tied((sent, halves, base), parts)
    two_left, two_right, one_left, one_right = parts
    zeros = jnp.zeros_like(halves[0])
    low, high = jnp.concatenate([halves[0], zeros], 0), jnp.concatenate([zeros, halves[1]], 0)
    to_right = (two_right + sent[0].astype(F32) + low.astype(F32)).astype(BF)
    to_left = (two_left + sent[1].astype(F32) + high.astype(F32)).astype(BF)
    to_right, to_left = z_shift(to_right, 1), z_shift(to_left, -1)
    to_right = (one_right + to_right.astype(F32)).astype(BF)
    to_left = (one_left + to_left.astype(F32)).astype(BF)
    move = z_shift if last else diagonal
    return base, move(to_right, 1), move(to_left, -1)


def pack(rollout, source):
    tokens = rollout.shape[1]
    place = lax.axis_index("dp")
    count = lax.axis_size("dp")
    blocks = [rollout]
    for hops in range(1, count):
        pairs = [(i, (i + hops) % count) for i in range(count)]
        blocks.append(lax.ppermute(rollout, "dp", pairs))
    ids = jnp.concatenate(
        [
            (place - hops) % count * tokens + jnp.arange(tokens, dtype=jnp.int32)
            for hops in range(count)
        ]
    )
    chosen = (ids[:, None] == source[None, :]).astype(BF)
    return jnp.dot(
        jnp.concatenate(blocks, axis=1), chosen, preferred_element_type=F32
    ).astype(BF)


def turn_in_body(idx, q_ref, kv_ref, other_q_ref, other_kv_ref, out_ref):
    half = HD // 2
    for base, q, kv in ((0, q_ref, kv_ref), (OWN, other_q_ref, other_kv_ref)):
        out_ref[0, base : base + QROWS, :] = q[...].T
        out_ref[0, base + QROWS : base + QROWS + half, :] = kv[0]
        out_ref[0, base + QROWS + half : base + OWN, :] = kv[1]


def turn_out_body(idx, own_ref, other_ref, out_ref):
    out_ref[0, :, 0:QROWS] = own_ref[...].T
    out_ref[0, :, QROWS:SHARD] = other_ref[...].T


def turn(body, idx, operands, specs, rows, cols):
    return pl.pallas_call(
        body,
        grid_spec=pltpu.PrefetchScalarGridSpec(
            num_scalar_prefetch=1,
            grid=(CHIPS,),
            in_specs=specs,
            out_specs=pl.BlockSpec((1, rows, cols), lambda i, idx: (i, 0, 0)),
        ),
        out_shape=jax.ShapeDtypeStruct((CHIPS, rows, cols), BF),
        compiler_params=pltpu.CompilerParams(vmem_limit_bytes=TURN_LIMIT * 2**20),
        cost_estimate=pl.CostEstimate(
            flops=0, bytes_accessed=4 * CHIPS * rows * cols, transcendentals=0
        ),
    )(idx, *operands)


def turn_in(idx, own, other):
    specs = [
        pl.BlockSpec((SHARD, QROWS), lambda i, idx: (2 * i + idx[CORE], 0)),
        pl.BlockSpec((2, HD // 2, SHARD), lambda i, idx: (0, 0, 2 * i + idx[CORE])),
    ]
    return turn(turn_in_body, idx, (*own, *other), specs * 2, ROWS, SHARD)


def turn_out(idx, own, other):
    spec = pl.BlockSpec((QROWS, SHARD), lambda i, idx: (0, 2 * i + idx[CORE]))
    return turn(turn_out_body, idx, (own, other), [spec] * 2, SHARD, SHARD)


def shards(rollout_acts, pack_source, segments, gain, wq, wkv, wo):
    section = lax.axis_index("section")
    count = lax.axis_size("section")
    z, core = lax.axis_index("z"), lax.axis_index("core")
    order = (z + jnp.array(ORDER, jnp.int32)) & (CHIPS - 1)

    def index(clock):
        rest = [(z >> 1) & 1, core, 1 - core, jnp.clip(clock - section, 0, MICRO - 1)]
        return jnp.concatenate([order, jnp.stack(rest)]).astype(jnp.int32)

    wq, wkv, wo = wq[0], wkv[0].transpose(0, 2, 1), wo[0]
    wq_other, wkv_other = sibling(wq), sibling(wkv)
    packed = pack(rollout_acts, pack_source[0].reshape(-1))
    packed = [packed[:, m * SEQ : (m + 1) * SEQ] for m in range(MICRO)]
    gains = jnp.broadcast_to(gain[0].astype(F32)[:, None], (SHARD, SEQ))
    seg = segments[0]
    spots = jnp.arange(SEQ, dtype=jnp.int32)
    mask = (
        (seg[:, :, None] == seg[:, None, :]) & (spots[:, None] <= spots[None, :])[None]
    ).astype(F32)
    taken = list(packed)
    clocks = MICRO + count - 1
    mirror = lambda v: lax.ppermute(v, "section", [(i, count - 1 - i) for i in range(count)])
    x = packed[0]
    payload = prepare(index(0), x, gains)
    (wo, wq_other, wkv_other), payload = tied((wo, wq_other, wkv_other), payload)
    w_in = turn_in(index(0), (wq, wkv), (wq_other, wkv_other))
    w_out = turn_out(index(0), wo, sibling(wo))
    for clock in range(clocks):
        for m in range(MICRO):
            if m < clock < m + count:
                taken[m] = jnp.where(section == clock - m, x, taken[m])
        last = clock == clocks - 1
        if last:
            mirrored = mirror(jnp.stack(taken))
            done = jnp.stack([jnp.where(section == 0, x, taken[0]), taken[1]])
            produced = along_section(done, -1)
        idx = index(clock)
        terms = layer(idx, x, payload, mask, w_in, w_out, last)
        if last or clock + 1 < MICRO:
            x = sum(term.astype(F32) for term in terms).astype(BF)
            if not last:
                x = jnp.where(section == 0, packed[clock + 1], x)
                payload = prepare(idx, x, gains)
        else:
            x, payload = combine(idx, *terms, gains)
    ending = jnp.where(section == count - 1, x, produced[1])
    return (jnp.stack([produced[0], ending])[None, None], mirrored[None, None])


def solution(mesh):
    devices = mesh.devices
    sections, ways, replicas = devices.shape
    fine = Mesh(devices.reshape(sections, ways // 2, 2, replicas), ("section", "z", "core", "dp"))
    tp = ("z", "core")
    in_specs = (
        P(tp, "dp"),
        P("dp", None, None),
        P("dp", None, None),
        P("section", tp),
        P("section", None, tp),
        P("section", None, None, tp),
        P("section", tp, None),
    )
    out_specs = (P("section", "dp", None, tp, None), P("section", "dp", None, tp, None))
    return jax.shard_map(shards, mesh=fine, in_specs=in_specs, out_specs=out_specs, check_vma=False)
```
